32 devices in a mesh: groups: 2 (over x), tile: 16 (over z, y, core).
Axes of the slice: x: 2, y: 2, z: 4, core: 2. Of those that a mesh axis runs over, the one named last changes fastest.
Arguments:
- queries: bfloat16 [2, 256, 8192], P(None, ('groups', 'tile')), parts along dimension 1, may hold values from -120 to 120
- fresh_kv: bfloat16 [2, 2, 256, 512], P(None, None, ('groups', 'tile')), parts along dimension 2, may hold values from -6 to 6
- cache: bfloat16 [2, 256, 512, 512], P(None, ('groups', 'tile')), parts along dimension 1, may hold values from -6 to 6
- lengths: int32 [256], P(('groups', 'tile')), parts along dimension 0, may hold values from 1 to 510, 16384 in all
- out_weight: bfloat16 [16, 1024, 8192], P('tile'), may hold values from -0.0625 to 0.0625
Outputs:
- projected: bfloat16 [2, 256, 16384], P(None, ('groups', 'tile')), parts along dimension 1
The draws below stay inside these ranges and needn't reach their ends.
There are 2 independent parts, one for each index of `groups`. The reference program is written for one: setup_inputs(seed, part) draws one part's arguments, and reference() takes and returns one part's arrays. A program takes and returns all parts, laid end to end along the dimension named above; an argument that names none is the same for every part. Nothing has to cross between parts.
Inputs may be any that keep to these rules, and one draw needn't show every extreme that they name: `lengths`: the longest request has exactly 510 cached tokens.
All inputs are finite; a program needn't handle non-finite values. No bound on the sum of `lengths` on one device may be relied on, other than what follows from the above.
Results may differ from the reference program's by a relative error of at most 0.0057.
Values may be sent and summed in bfloat16 or wider, within the bound.
No kernel may reach another device: no remote copies, remote signals or barrier semaphores. Data moves between devices by JAX's collectives and lax.ppermute only.
A program may use at most 128 MiB of HBM per device.

```python
import math
import jax
import jax.numpy as jnp
import numpy as np
from jax import lax

QH = 64
KVH = 4
HD = 128
DM = 16384
DECODE_STEPS = 2
GRID_ROWS = 8
CAP = 512
REQS = 128
GRID_COLS = 2
ROW_W = 1024
COL_W = 8192
N_TILE = 16


def draw_cache(key, part):
    key = jax.random.fold_in(key, 3)
    values = jax.random.normal(key, (2, REQS, CAP, KVH * HD), jnp.float32)
    return jnp.clip(values, -6.0, 6.0).astype(jnp.bfloat16)


def draw_queries(key, part):
    key = jax.random.fold_in(key, 5)
    shape = (DECODE_STEPS, REQS, KVH, QH // KVH, HD)
    base = jnp.clip(jax.random.normal(key, shape, jnp.float32), -6.0, 6.0)
    return base.reshape(DECODE_STEPS, REQS, QH * HD).astype(jnp.bfloat16)


def block_levels(key, dims, split, least, top_value):
    gain = 1.0
    for dim, parts in split:
        draws = jax.random.uniform(jax.random.fold_in(jax.random.fold_in(key, 6), dim), (parts,), jnp.float32, least / len(split), top_value / len(split))
        gain = gain * jnp.repeat(jnp.exp(draws), dims[dim] // parts).reshape((-1,) + (1,) * (len(dims) - 1 - dim))
    return gain


def split_up(count, total, most, slope):
    loads = [(1 << 20) // math.isqrt(rank ** slope) + 1 for rank in range(2, count + 1)]
    spare, given = total - most - (count - 1), [1] * (count - 1)
    while spare > 0:
        free = [i for i in range(count - 1) if given[i] < most]
        whole, budget = sum([loads[i] for i in free]), spare
        for i in free:
            more = min(most - given[i], max(1, budget * loads[i] // whole), spare)
            given[i] = given[i] + more
            spare = spare - more
    return np.array([most] + given)


def uneven(own_key, count, total, limit, slope):
    if count == 2:
        one = jax.random.randint(own_key, (), max(1, total - limit), min(limit, total - 1) + 1)
        return jnp.stack([one, total - one])
    sizes = jnp.asarray(split_up(count, total, limit, slope), jnp.int32)
    twos = (count - 1) // 2
    source_of, receiver = sizes[1:1 + 2 * twos:2], sizes[2:2 + 2 * twos:2]
    slack = jnp.minimum(source_of - 1, limit - receiver)
    moved = jax.random.randint(jax.random.fold_in(own_key, 1), (twos,), 0, 1 << 20) % (slack + 1)
    sizes = sizes.at[1:1 + 2 * twos:2].set(source_of - moved).at[2:2 + 2 * twos:2].set(receiver + moved)
    return sizes[jax.random.permutation(jax.random.fold_in(own_key, 2), count)]


def centred(stream_key, dims, width, reach, pieces=(), held_as=jnp.bfloat16):
    array = jax.random.normal(stream_key, dims, jnp.float32) * width
    if len(pieces) > 0:
        array = block_levels(stream_key, dims, pieces, -0.22, 0.18) * array
    return jnp.clip(array, min=-reach, max=reach).astype(held_as)


def setup_inputs(seed: int = 0, part: int = 0) -> dict:
    streams_of = jax.random.split(jax.random.key(seed), 6)
    part_splits = jax.random.split(jax.random.fold_in(streams_of[5], part), 6)
    return {
        "queries": draw_queries(jax.random.fold_in(jax.random.fold_in(streams_of[5], part), 71), part),
        "fresh_kv": centred(part_splits[1], (DECODE_STEPS, 2, REQS, KVH * HD), 1.0, 6.0, ((2, 16),)),
        "cache": draw_cache(jax.random.fold_in(jax.random.fold_in(streams_of[5], part), 71), part),
        "lengths": uneven(part_splits[3], REQS, REQS * CAP // 4, CAP - 2, 2).astype(jnp.int32),
        "out_weight": centred(streams_of[4], (N_TILE, ROW_W, COL_W), (QH * HD) ** -0.5, 0.0625, ((0, 16),)),
    }


def attend_request(query, cache_keys, cache_values, fresh_keys, fresh_values, length):
    factor = 1.0 / math.sqrt(HD)
    cached_scores = jnp.einsum('kgd,ckd->kgc', query, cache_keys) * factor
    positions = jnp.arange(CAP)
    visible = positions < length
    cached_scores = jnp.where(visible[None, None, :], cached_scores, -jnp.inf)
    fresh_scores = jnp.einsum('kgd,skd->kgs', query, fresh_keys) * factor
    top = jnp.maximum(cached_scores.max(-1), fresh_scores.max(-1))[..., None]
    cached_exp = jnp.exp(cached_scores - top)
    fresh_exp = jnp.exp(fresh_scores - top)
    total = cached_exp.sum(-1, keepdims=True) + fresh_exp.sum(-1, keepdims=True)
    cached_weights = (cached_exp / total).astype(jnp.bfloat16).astype(jnp.float32)
    fresh_weights = (fresh_exp / total).astype(jnp.bfloat16).astype(jnp.float32)
    mixed = jnp.einsum('kgc,ckd->kgd', cached_weights, cache_values)
    mixed = mixed + jnp.einsum('kgs,skd->kgd', fresh_weights, fresh_values)
    return mixed.astype(jnp.bfloat16)

def assemble(out_weight):
    tiles = out_weight.reshape(GRID_COLS, GRID_ROWS, ROW_W, COL_W)
    return jnp.transpose(tiles, (1, 2, 0, 3)).reshape(QH * HD, DM)

def reference(queries, fresh_kv, cache, lengths, out_weight):
    per_group = QH // KVH
    matrix = assemble(out_weight)
    results = []
    for step_index in range(DECODE_STEPS):
        seen = step_index + 1
        query_all = queries[step_index].reshape(REQS, KVH, per_group, HD)
        fresh_keys = fresh_kv[:seen, 0].reshape(seen, REQS, KVH, HD)
        fresh_values = fresh_kv[:seen, 1].reshape(seen, REQS, KVH, HD)

        def one_request(index):
            query = query_all[index].astype(jnp.float32)
            cache_keys = cache[0, index].reshape(CAP, KVH, HD).astype(jnp.float32)
            cache_values = cache[1, index].reshape(CAP, KVH, HD).astype(jnp.float32)
            new_keys = fresh_keys[:, index].astype(jnp.float32)
            new_values = fresh_values[:, index].astype(jnp.float32)
            return attend_request(query, cache_keys, cache_values, new_keys, new_values, lengths[index])
        attended = lax.map(one_request, jnp.arange(REQS, dtype=jnp.int32))
        attended = attended.reshape(REQS, QH * HD)
        results.append(jnp.dot(attended, matrix, preferred_element_type=jnp.float32).astype(jnp.bfloat16))
    return jnp.stack(results)
```

```python
import functools
import math

import jax
import jax.numpy as jnp
from jax import lax
from jax.experimental import pallas as pl
from jax.experimental.pallas import tpu as pltpu
from jax.sharding import PartitionSpec as P

QH = 64
KVH = 4
HD = 128
DECODE_STEPS = 2
GRID_ROWS = 8
GROUP = QH // KVH
BLOCK_HEADS = QH // GRID_ROWS
CHUNKS = 2
TILE_N = 512
MIB = 1 << 20


def attention_kernel(lengths_ref, query_ref, fresh_ref, cache_ref, out_ref, cached, sems):
    slots, capacity = cached.shape[1], cached.shape[2]
    factor = 1.0 / math.sqrt(HD)
    rows = DECODE_STEPS * GROUP

    def copy(which, slot):
        return pltpu.make_async_copy(
            cache_ref.at[which, slot], cached.at[which, slot], sems.at[which, slot]
        )

    for slot in range(slots):
        for which in range(2):
            copy(which, slot).start()
    position = lax.broadcasted_iota(jnp.int32, (rows, capacity), 1)
    step = lax.broadcasted_iota(jnp.int32, (rows, capacity), 0) // GROUP
    window_row = lax.broadcasted_iota(jnp.int32, (32, cached.shape[3]), 0)
    for slot in range(slots):
        length = lengths_ref[slot]
        base = pl.multiple_of(jnp.minimum((length // 16) * 16, capacity - 32), 16)
        for which in range(2):
            copy(which, slot).wait()
            window = cached[which, slot, pl.ds(base, 32), :].astype(jnp.float32)
            for t in range(DECODE_STEPS):
                fresh = fresh_ref[t, which].astype(jnp.float32)[slot : slot + 1]
                window = jnp.where(window_row + base == length + t, fresh, window)
            cached[which, slot, pl.ds(base, 32), :] = window.astype(jnp.bfloat16)
        visible = position < length + 1 + step
        for head in range(KVH):
            lanes = slice(head * HD, (head + 1) * HD)
            scores = lax.dot_general(
                query_ref[slot, head],
                cached[0, slot, :, lanes],
                (((1,), (1,)), ((), ())),
                preferred_element_type=jnp.float32,
            )
            scores = jnp.where(visible, scores * factor, -jnp.inf)
            weights = jnp.exp(scores - scores.max(-1, keepdims=True))
            weights = weights / weights.sum(-1, keepdims=True)
            mixed = jnp.dot(
                weights.astype(jnp.bfloat16),
                cached[1, slot, :, lanes],
                preferred_element_type=jnp.float32,
            )
            out_ref[slot, head] = mixed.astype(jnp.bfloat16)


def attend(queries, fresh_kv, cache, lengths):
    slots, capacity, width = cache.shape[1:]
    rows = DECODE_STEPS * GROUP
    query = queries.reshape(DECODE_STEPS, slots, KVH, GROUP, HD)
    query = jnp.transpose(query, (1, 2, 0, 3, 4)).reshape(slots, KVH, rows, HD)
    vmem = pl.BlockSpec(memory_space=pltpu.VMEM)
    return pl.pallas_call(
        attention_kernel,
        out_shape=jax.ShapeDtypeStruct((slots, KVH, rows, HD), jnp.bfloat16),
        in_specs=[
            pl.BlockSpec(memory_space=pltpu.SMEM),
            vmem,
            vmem,
            pl.BlockSpec(memory_space=pl.ANY),
        ],
        out_specs=vmem,
        scratch_shapes=[
            pltpu.VMEM((2, slots, capacity, width), jnp.bfloat16),
            pltpu.SemaphoreType.DMA((2, slots)),
        ],
        compiler_params=pltpu.CompilerParams(vmem_limit_bytes=32 * MIB),
        name="attention",
    )(lengths, query, fresh_kv, cache)


def project_kernel(place_ref, x_ref, w_ref, fg_ref, fk_ref, ng_ref, nk_ref, ordered):
    devices, _, slot_rows, _ = x_ref.shape
    cols = devices // GRID_ROWS
    far = GRID_ROWS * (cols - 1) * slot_rows

    def place(source, row):
        for head in range(BLOCK_HEADS):
            ordered[row : row + slot_rows, head * HD : (head + 1) * HD] = x_ref[source, head]

    @pl.when(pl.program_id(0) == 0)
    def _():
        own_block, own_row = place_ref[0], place_ref[1]
        order = [0, 2, 4, 6, 1, 3, 5, 7]
        for index, distance in enumerate(order):
            row = jnp.bitwise_xor(own_row, distance)
            for shift in range(1, cols):
                block = lax.rem(own_block + shift, cols)
                place(block * GRID_ROWS + row, (index * (cols - 1) + shift - 1) * slot_rows)
            place(own_block * GRID_ROWS + row, far + index * slot_rows)

    product = jnp.dot(ordered[...], w_ref[0], preferred_element_type=jnp.float32)
    product = product.astype(jnp.bfloat16)
    half = far // 2
    fk_ref[...] = product[:half].reshape(fk_ref.shape)
    fg_ref[...] = product[half:far].reshape(fg_ref.shape)
    nk_ref[...] = product[far : far + slot_rows * 4].reshape(nk_ref.shape)
    ng_ref[...] = product[far + slot_rows * 4 :].reshape(ng_ref.shape)


def project(x, place, out_weight, chunk, chunks):
    devices, _, slot_rows, _ = x.shape
    cols = devices // GRID_ROWS
    width = out_weight.shape[2] // chunks
    tile = min(TILE_N, width)
    steps = width // tile
    far = (4, (cols - 1) * slot_rows, width)
    near = (4, slot_rows, width)

    def spec(shape):
        return pl.BlockSpec(shape[:2] + (tile,), lambda i, place: (0, 0, i))

    return pl.pallas_call(
        project_kernel,
        grid_spec=pltpu.PrefetchScalarGridSpec(
            num_scalar_prefetch=1,
            grid=(steps,),
            in_specs=[
                pl.BlockSpec(x.shape, lambda i, place: (0, 0, 0, 0)),
                pl.BlockSpec(
                    (1, out_weight.shape[1], tile), lambda i, place: (0, 0, chunk * steps + i)
                ),
            ],
            out_specs=[spec(far), spec(far), spec(near), spec(near)],
            scratch_shapes=[pltpu.VMEM((devices * slot_rows, BLOCK_HEADS * HD), jnp.bfloat16)],
        ),
        out_shape=[jax.ShapeDtypeStruct(s, jnp.bfloat16) for s in (far, far, near, near)],
        compiler_params=pltpu.CompilerParams(vmem_limit_bytes=40 * MIB),
        name="project",
    )(place, x, out_weight)


def swap(value, distance):
    devices = lax.axis_size("tile")
    return lax.ppermute(value, "tile", [(i, i ^ distance) for i in range(devices)])


def add(kept, arrived):
    return kept.astype(jnp.float32) + arrived.astype(jnp.float32)


def reduce_square(give, keep):
    half = give.shape[2] // 2
    total = add(keep, swap(give, 1)).astype(jnp.bfloat16)
    left, right = total[..., :half], total[..., half:]
    left = left.reshape((2, 2) + left.shape[1:])
    right = right.reshape((2, 2) + right.shape[1:])
    left = add(left[:, 0], swap(left[:, 1], 2)).astype(jnp.bfloat16)
    right = add(right[0], swap(right[1], 4)).astype(jnp.bfloat16)
    left = add(left[0], swap(left[1], 4)).astype(jnp.bfloat16)
    right = add(right[0], swap(right[1], 2)).astype(jnp.bfloat16)
    return jnp.concatenate([left, right], axis=-1)


def per_device(queries, fresh_kv, cache, lengths, out_weight):
    slots = cache.shape[1]
    devices = lax.axis_size("tile")
    cols = devices // GRID_ROWS
    col_width = out_weight.shape[2]
    slot_rows = DECODE_STEPS * slots
    own = lax.axis_index("tile")
    own_block, own_row = own // GRID_ROWS, own % GRID_ROWS

    attended = attend(queries, fresh_kv, cache, lengths)
    blocks = attended.reshape(slots, KVH, DECODE_STEPS, GROUP // BLOCK_HEADS, BLOCK_HEADS, HD)
    blocks = jnp.transpose(blocks, (1, 3, 4, 2, 0, 5))
    blocks = blocks.reshape(GRID_ROWS, BLOCK_HEADS, slot_rows, HD)
    outgoing = jnp.broadcast_to(blocks[None], (cols,) + blocks.shape)
    outgoing = outgoing.reshape((devices,) + blocks.shape[1:])
    arrived = lax.all_to_all(outgoing, "tile", split_axis=0, concat_axis=0, tiled=True)

    place = jnp.stack([own_block, own_row]).astype(jnp.int32)
    pieces = []
    for chunk in range(CHUNKS):
        far_give, far_keep, near_give, near_keep = project(
            arrived, place, out_weight, chunk, CHUNKS
        )
        far = reduce_square(far_give, far_keep).reshape(cols - 1, slot_rows, -1)
        near = reduce_square(near_give, near_keep)
        back = [near]
        for shift in range(1, cols):
            targets = [
                (i, (i // GRID_ROWS + shift) % cols * GRID_ROWS + i % GRID_ROWS)
                for i in range(devices)
            ]
            back.append(lax.ppermute(far[shift - 1], "tile", targets))
        pieces.append(jnp.stack(back))
    stacked = jnp.concatenate(pieces, axis=-1)
    blocks = [
        lax.dynamic_index_in_dim(stacked, lax.rem(own_block - j + cols, cols), 0, False)
        for j in range(cols)
    ]
    return jnp.concatenate(blocks, axis=-1).reshape(DECODE_STEPS, slots, cols * col_width)


def solution(mesh):
    return jax.shard_map(
        per_device,
        mesh=mesh,
        in_specs=(
            P(None, ("groups", "tile"), None),
            P(None, None, ("groups", "tile"), None),
            P(None, ("groups", "tile"), None, None),
            P(("groups", "tile")),
            P("tile", None, None),
        ),
        out_specs=P(None, ("groups", "tile"), None),
        check_vma=False,
    )
```

```python
import functools
import math

import jax
import jax.numpy as jnp
from jax import lax
from jax.experimental import pallas as pl
from jax.experimental.pallas import tpu as pltpu
from jax.sharding import PartitionSpec as P

QH = 64
KVH = 4
HD = 128
DECODE_STEPS = 2
GRID_ROWS = 8
GROUP = QH // KVH
BLOCK_HEADS = QH // GRID_ROWS
CHUNKS = 2
TILE_N = 1024
PAGE = 128
MIB = 1 << 20


def attention_kernel(lengths_ref, query_ref, fresh_ref, cache_ref, out_ref, cached, sems):
    slots, capacity, width = cached.shape[1:]
    factor = 1.0 / math.sqrt(HD)
    rows = KVH * DECODE_STEPS * GROUP
    head_rows = rows // KVH
    pages = capacity // PAGE

    def copies(slot, act):
        used = (lengths_ref[slot] + DECODE_STEPS + PAGE - 1) // PAGE
        used = jnp.where(used >= 3, pages, used)
        for page in range(pages):

            @pl.when(page < used)
            def _(page=page):
                span = pl.ds(page * PAGE, PAGE)
                for which in range(2):
                    act(
                        pltpu.make_async_copy(
                            cache_ref.at[which, slot, span],
                            cached.at[which, slot, span],
                            sems.at[which, slot, page],
                        )
                    )

        return used

    for slot in range(slots):
        copies(slot, lambda copy: copy.start())
    own = (
        lax.broadcasted_iota(jnp.int32, (rows, width), 0) // head_rows
        == lax.broadcasted_iota(jnp.int32, (rows, width), 1) // HD
    )
    window_row = lax.broadcasted_iota(jnp.int32, (32, width), 0)

    def mix(slot, count):
        position = lax.broadcasted_iota(jnp.int32, (rows, count), 1)
        step = lax.broadcasted_iota(jnp.int32, (rows, count), 0) // GROUP % DECODE_STEPS
        query = jnp.concatenate([query_ref[slot]] * KVH, axis=1)
        query = jnp.where(own, query, jnp.zeros((), query.dtype))
        scores = lax.dot_general(
            query,
            cached[0, slot, :count, :],
            (((1,), (1,)), ((), ())),
            preferred_element_type=jnp.float32,
        )
        visible = position < lengths_ref[slot] + 1 + step
        scores = jnp.where(visible, scores * factor, -jnp.inf)
        weights = jnp.exp(scores - scores.max(-1, keepdims=True))
        weights = weights * (1.0 / weights.sum(-1, keepdims=True))
        mixed = jnp.dot(
            weights.astype(jnp.bfloat16),
            cached[1, slot, :count, :],
            preferred_element_type=jnp.float32,
        )
        for head in range(KVH):
            own_rows = slice(head * head_rows, (head + 1) * head_rows)
            own_lanes = slice(head * HD, (head + 1) * HD)
            out_ref[slot, own_rows, :] = mixed[own_rows, own_lanes].astype(jnp.bfloat16)

    for slot in range(slots):
        used = copies(slot, lambda copy: copy.wait())
        length = lengths_ref[slot]
        base = pl.multiple_of(jnp.minimum((length // 16) * 16, capacity - 32), 16)
        for which in range(2):
            window = cached[which, slot, pl.ds(base, 32), :].astype(jnp.float32)
            for t in range(DECODE_STEPS):
                fresh = fresh_ref[t, which].astype(jnp.float32)[slot : slot + 1]
                window = jnp.where(window_row + base == length + t, fresh, window)
            cached[which, slot, pl.ds(base, 32), :] = window.astype(jnp.bfloat16)
        for count in (1, 2, pages):
            pl.when(used == count)(functools.partial(mix, slot, count * PAGE))


def attend(queries, fresh_kv, cache, lengths):
    slots, capacity, width = cache.shape[1:]
    rows = KVH * DECODE_STEPS * GROUP
    query = queries.reshape(DECODE_STEPS, slots, KVH, GROUP, HD)
    query = jnp.transpose(query, (1, 2, 0, 3, 4)).reshape(slots, rows, HD)
    vmem = pl.BlockSpec(memory_space=pltpu.VMEM)
    return pl.pallas_call(
        attention_kernel,
        out_shape=jax.ShapeDtypeStruct((slots, rows, HD), jnp.bfloat16),
        in_specs=[
            pl.BlockSpec(memory_space=pltpu.SMEM),
            vmem,
            vmem,
            pl.BlockSpec(memory_space=pl.ANY),
        ],
        out_specs=vmem,
        scratch_shapes=[
            pltpu.VMEM((2, slots, capacity, width), jnp.bfloat16),
            pltpu.SemaphoreType.DMA((2, slots, capacity // PAGE)),
        ],
        compiler_params=pltpu.CompilerParams(vmem_limit_bytes=53 * MIB),
        name="attention",
    )(lengths, query, fresh_kv, cache)


def load_kernel(source_ref, *refs):
    out_refs, sems = refs[:-1], refs[-1]
    width = out_refs[0].shape[1]
    rows = source_ref.shape[1] // sems.shape[1]
    copies = [
        pltpu.make_async_copy(
            source_ref.at[0, pl.ds(i * rows, rows), pl.ds(chunk * width, width)],
            out_ref.at[pl.ds(i * rows, rows)],
            sems.at[chunk, i],
        )
        for chunk, out_ref in enumerate(out_refs)
        for i in range(sems.shape[1])
    ]
    for copy in copies:
        copy.start()
    for copy in copies:
        copy.wait()


def load(weight, chunks):
    _, depth, width = weight.shape
    shape = jax.ShapeDtypeStruct((depth, width // chunks), weight.dtype)
    return pl.pallas_call(
        load_kernel,
        in_specs=[pl.BlockSpec(memory_space=pl.ANY)],
        out_specs=[pl.BlockSpec(memory_space=pl.ANY)] * chunks,
        out_shape=[shape] * chunks,
        scratch_shapes=[pltpu.SemaphoreType.DMA((chunks, 4))],
        compiler_params=pltpu.CompilerParams(vmem_limit_bytes=36 * MIB),
        cost_estimate=pl.CostEstimate(flops=0, bytes_accessed=4 * weight.size, transcendentals=0),
        name="load",
    )(weight)


def project_kernel(*refs):
    x_refs, w_ref = refs[:8], refs[8]
    out_refs, ordered = refs[9:13], refs[13]
    depth, width = w_ref.shape
    tile = min(TILE_N, width)
    row = 0
    for group in (x_refs[:4], x_refs[4:]):
        shifts, _, _, slot_rows, _ = group[0].shape
        for core in range(2):
            for x_ref in group:
                for shift in range(shifts):
                    for head in range(BLOCK_HEADS):
                        ordered[row : row + slot_rows, head * HD : (head + 1) * HD] = x_ref[
                            shift, core, head
                        ]
                    row += slot_rows
    for start in range(0, width, tile):
        lanes = slice(start, start + tile)
        product = jnp.dot(ordered[...], w_ref[:, lanes], preferred_element_type=jnp.float32)
        product = product.astype(jnp.bfloat16)
        row = 0
        for out_ref in out_refs:
            count = out_ref.shape[0] * out_ref.shape[1]
            out_ref[:, :, lanes] = product[row : row + count].reshape(out_ref.shape[:2] + (tile,))
            row += count


def project(far, near, weight):
    shifts, _, _, slot_rows, _ = far[0].shape
    depth, width = weight.shape
    rows = 8 * (shifts + 1) * slot_rows
    far_shape = jax.ShapeDtypeStruct((4, shifts * slot_rows, width), jnp.bfloat16)
    near_shape = jax.ShapeDtypeStruct((4, slot_rows, width), jnp.bfloat16)
    vmem = pl.BlockSpec(memory_space=pltpu.VMEM)
    return pl.pallas_call(
        project_kernel,
        in_specs=[vmem] * 9,
        out_specs=[vmem] * 4,
        scratch_shapes=[pltpu.VMEM((rows, depth), jnp.bfloat16)],
        out_shape=[far_shape] * 2 + [near_shape] * 2,
        compiler_params=pltpu.CompilerParams(vmem_limit_bytes=8 * MIB),
        cost_estimate=pl.CostEstimate(
            flops=2 * rows * depth * width,
            bytes_accessed=2 * depth * width,
            transcendentals=0,
        ),
        name="project",
    )(*far, *near, weight)


def swap(value, distance):
    devices = lax.axis_size("tile")
    return lax.ppermute(value, "tile", [(i, i ^ distance) for i in range(devices)])


def widen(value):
    return value.astype(jnp.float32)


def direct(total):
    sent = total.astype(jnp.bfloat16)
    arrived = [swap(sent[i], 2 * i) for i in range(1, 4)]
    return total[0] + sum(widen(value) for value in arrived)


def per_device(queries, fresh_kv, cache, lengths, out_weight):
    slots = cache.shape[1]
    devices = lax.axis_size("tile")
    cols = devices // GRID_ROWS
    col_width = out_weight.shape[2]
    slot_rows = DECODE_STEPS * slots
    own = lax.axis_index("tile")
    own_block = own // GRID_ROWS
    own_square = own // 2 % 4
    own_core = own % 2

    def send(value, shift, distance):
        def target(i):
            block, row = i // GRID_ROWS, i % GRID_ROWS
            return (block + shift) % cols * GRID_ROWS + (row ^ distance)

        return lax.ppermute(value, "tile", [(i, target(i)) for i in range(devices)])

    attended = attend(queries, fresh_kv, cache, lengths)
    blocks = attended.reshape(slots, KVH, DECODE_STEPS, GROUP // BLOCK_HEADS, BLOCK_HEADS, HD)
    blocks = jnp.transpose(blocks, (3, 1, 4, 2, 0, 5))
    blocks = blocks.reshape(2, 4, BLOCK_HEADS, slot_rows, HD)
    kept = jnp.where(own_core == 0, blocks[0], blocks[1])
    given = jnp.where(own_core == 0, blocks[1], blocks[0])
    cat = jnp.stack([kept, swap(given, 1)], axis=1)
    cat, weight = lax.optimization_barrier((cat, out_weight))
    cat = [
        lax.dynamic_index_in_dim(cat, jnp.bitwise_xor(own_square, distance), 0, False)
        for distance in range(4)
    ]
    far = [
        jnp.stack([send(cat[i], shift, 2 * i) for shift in range(1, cols)]) for i in range(4)
    ]
    near = [(send(cat[i], 0, 2 * i) if i else cat[0])[None] for i in range(4)]
    weights = load(weight, CHUNKS)
    partial = [project(far, near, weight) for weight in weights]
    near_total = jnp.concatenate(
        [widen(keep) + widen(swap(give, 1)) for _, _, keep, give in partial], axis=-1
    )
    backs = []
    for chunk, (keep, give, _, _) in enumerate(partial):
        sums = direct(widen(keep) + widen(swap(give, 1))).astype(jnp.bfloat16)
        if chunk == 0:
            sums, near_total = lax.optimization_barrier((sums, near_total))
        sums = sums.reshape(cols - 1, slot_rows, -1)
        backs.append(jnp.stack([send(sums[s - 1], cols - s, 0) for s in range(1, cols)]))
    near = direct(near_total).astype(jnp.bfloat16)
    stacked = jnp.concatenate([near[None], jnp.concatenate(backs, axis=-1)])
    blocks = [
        lax.dynamic_index_in_dim(stacked, lax.rem(j - own_block + cols, cols), 0, False)
        for j in range(cols)
    ]
    return jnp.concatenate(blocks, axis=-1).reshape(DECODE_STEPS, slots, cols * col_width)


def solution(mesh):
    return jax.shard_map(
        per_device,
        mesh=mesh,
        in_specs=(
            P(None, ("groups", "tile"), None),
            P(None, None, ("groups", "tile"), None),
            P(None, ("groups", "tile"), None, None),
            P(("groups", "tile")),
            P("tile", None, None),
        ),
        out_specs=P(None, ("groups", "tile"), None),
        check_vma=False,
    )
```

```python
import functools
import math

import jax
import jax.numpy as jnp
from jax import lax
from jax.experimental import pallas as pl
from jax.experimental.pallas import tpu as pltpu
from jax.sharding import PartitionSpec as P

QH = 64
KVH = 4
HD = 128
DECODE_STEPS = 2
GRID_ROWS = 8
GROUP = QH // KVH
BLOCK_HEADS = QH // GRID_ROWS
CHUNKS = 2
TILE_N = 1024
PAGE = 128
TOGETHER = 4
NEAR_GRANT = 24
MIB = 1 << 20


def attention_kernel(
    lengths_ref, query_ref, fresh_ref, cache_ref, out_ref, cached, lengths, fresh, sems, small_sems
):
    slots, capacity, width = cached.shape[1:]
    factor = 1.0 / math.sqrt(HD)
    rows = KVH * DECODE_STEPS * GROUP
    head_rows = rows // KVH
    pages = capacity // PAGE

    def copy(which, slot, page):
        span = pl.ds(page * PAGE, PAGE)
        return pltpu.make_async_copy(
            cache_ref.at[which, slot, span], cached.at[which, slot, span], sems.at[which, slot, page]
        )

    def page_copies(slot, first, used, act):
        for page in range(first, pages):

            @pl.when(page < used)
            def _(page=page):
                for which in range(2):
                    act(copy(which, slot, page))

    lengths_copy = pltpu.make_async_copy(lengths_ref, lengths, small_sems.at[0])
    fresh_copy = pltpu.make_async_copy(fresh_ref, fresh, small_sems.at[1])
    lengths_copy.start()
    fresh_copy.start()
    for slot in range(slots):
        for which in range(2):
            copy(which, slot, 0).start()
    lengths_copy.wait()

    def used_pages(group):
        longest = lengths[group[0]]
        for slot in group[1:]:
            longest = jnp.maximum(longest, lengths[slot])
        used = (longest + DECODE_STEPS + PAGE - 1) // PAGE
        return jnp.where(used >= 3, pages, used)

    groups = [range(first, first + TOGETHER) for first in range(0, slots, TOGETHER)]
    for group in groups:
        used = used_pages(group)
        for slot in group:
            page_copies(slot, 1, used, lambda copy: copy.start())
    own = (
        lax.broadcasted_iota(jnp.int32, (rows, width), 0) // head_rows
        == lax.broadcasted_iota(jnp.int32, (rows, width), 1) // HD
    )
    window_row = lax.broadcasted_iota(jnp.int32, (32, width), 0)
    fresh_copy.wait()

    def patch(slot):
        length = lengths[slot]
        base = pl.multiple_of(jnp.minimum((length // 16) * 16, capacity - 32), 16)
        for which in range(2):
            window = cached[which, slot, pl.ds(base, 32), :].astype(jnp.float32)
            for t in range(DECODE_STEPS):
                row = fresh[t, which].astype(jnp.float32)[slot : slot + 1]
                window = jnp.where(window_row + base == length + t, row, window)
            cached[which, slot, pl.ds(base, 32), :] = window.astype(jnp.bfloat16)

    def mix(group, count):
        position = lax.broadcasted_iota(jnp.int32, (rows, count), 1)
        step = lax.broadcasted_iota(jnp.int32, (rows, count), 0) // GROUP % DECODE_STEPS
        visible = position - step
        scores = []
        for slot in group:
            query = jnp.concatenate([query_ref[slot]] * KVH, axis=1)
            query = jnp.where(own, query, jnp.zeros((), query.dtype))
            scores.append(
                lax.dot_general(
                    query,
                    cached[0, slot, :count, :],
                    (((1,), (1,)), ((), ())),
                    preferred_element_type=jnp.float32,
                )
            )
        weights = []
        for slot, score in zip(group, scores):
            score = jnp.where(visible <= lengths[slot], score * factor, -jnp.inf)
            weight = jnp.exp(score - score.max(-1, keepdims=True))
            weights.append(weight * (1.0 / weight.sum(-1, keepdims=True)))
        for slot, weight in zip(group, weights):
            mixed = jnp.dot(
                weight.astype(jnp.bfloat16),
                cached[1, slot, :count, :],
                preferred_element_type=jnp.float32,
            )
            for head in range(KVH):
                own_rows = slice(head * head_rows, (head + 1) * head_rows)
                own_lanes = slice(head * HD, (head + 1) * HD)
                out_ref[slot, own_rows, :] = mixed[own_rows, own_lanes].astype(jnp.bfloat16)

    for group in groups:
        used = used_pages(group)
        for slot in group:
            for which in range(2):
                copy(which, slot, 0).wait()
            page_copies(slot, 1, used, lambda copy: copy.wait())
        for slot in group:
            patch(slot)
        for count in (1, 2, pages):
            pl.when(used == count)(functools.partial(mix, group, count * PAGE))


def in_hbm(array):
    return pltpu.with_memory_space_constraint(array, pltpu.HBM)


def attend(queries, fresh_kv, cache, lengths):
    slots, capacity, width = cache.shape[1:]
    rows = KVH * DECODE_STEPS * GROUP
    query = queries.reshape(DECODE_STEPS, slots, KVH, GROUP, HD)
    query = jnp.transpose(query, (1, 2, 0, 3, 4)).reshape(slots, rows, HD)
    vmem = pl.BlockSpec(memory_space=pltpu.VMEM)
    hbm = pl.BlockSpec(memory_space=pltpu.HBM)
    return pl.pallas_call(
        attention_kernel,
        out_shape=jax.ShapeDtypeStruct((slots, rows, HD), jnp.bfloat16),
        in_specs=[hbm, vmem, hbm, hbm],
        out_specs=vmem,
        scratch_shapes=[
            pltpu.VMEM((2, slots, capacity, width), jnp.bfloat16),
            pltpu.SMEM(lengths.shape, lengths.dtype),
            pltpu.VMEM(fresh_kv.shape, fresh_kv.dtype),
            pltpu.SemaphoreType.DMA((2, slots, capacity // PAGE)),
            pltpu.SemaphoreType.DMA((2,)),
        ],
        compiler_params=pltpu.CompilerParams(vmem_limit_bytes=40 * MIB),
        name="attention",
    )(in_hbm(lengths), query, in_hbm(fresh_kv), in_hbm(cache))


def order_rows(x_refs, ordered):
    row = 0
    for core in range(2):
        for x_ref in x_refs:
            shifts, _, _, slot_rows, _ = x_ref.shape
            for shift in range(shifts):
                for head in range(BLOCK_HEADS):
                    ordered[row : row + slot_rows, head * HD : (head + 1) * HD] = x_ref[
                        shift, core, head
                    ]
                row += slot_rows


def multiply(ordered, w_ref, start, tile, out_refs, first):
    product = jnp.dot(
        ordered[...], w_ref[:, start : start + tile], preferred_element_type=jnp.float32
    ).astype(jnp.bfloat16)
    half = ordered.shape[0] // 2
    for i, out_ref in enumerate(out_refs):
        out_ref[:, :, first : first + tile] = product[i * half : (i + 1) * half].reshape(
            out_ref.shape[:2] + (tile,)
        )


def near_kernel(*refs):
    x_refs, source_ref = refs[:4], refs[4]
    out_refs, held_ref, ordered, sems = refs[5:7], refs[7], refs[8], refs[9]
    width = held_ref.shape[1]
    tile = width // sems.shape[0]

    def copy(i):
        span = pl.ds(i * tile, tile)
        return pltpu.make_async_copy(source_ref.at[0, :, span], held_ref.at[:, span], sems.at[i])

    for i in range(sems.shape[0]):
        copy(i).start()
    order_rows(x_refs, ordered)
    for i in range(sems.shape[0]):
        copy(i).wait()
        multiply(ordered, held_ref, i * tile, tile, out_refs, i * tile)


def project_near(pieces, weight):
    shifts, _, _, slot_rows, _ = pieces[0].shape
    _, depth, width = weight.shape
    shape = jax.ShapeDtypeStruct((4, shifts * slot_rows, width), jnp.bfloat16)
    vmem = pl.BlockSpec(memory_space=pltpu.VMEM)
    return pl.pallas_call(
        near_kernel,
        in_specs=[vmem] * 4 + [pl.BlockSpec(memory_space=pl.ANY)],
        out_specs=[vmem] * 3,
        scratch_shapes=[
            pltpu.VMEM((8 * shifts * slot_rows, depth), jnp.bfloat16),
            pltpu.SemaphoreType.DMA((max(1, width // TILE_N),)),
        ],
        out_shape=[shape] * 2 + [jax.ShapeDtypeStruct((depth, width), weight.dtype)],
        compiler_params=pltpu.CompilerParams(vmem_limit_bytes=NEAR_GRANT * MIB),
        cost_estimate=pl.CostEstimate(
            flops=16 * shifts * slot_rows * depth * width,
            bytes_accessed=4 * depth * width,
            transcendentals=0,
        ),
        name="project_near",
    )(*pieces, in_hbm(weight))


def far_kernel(*refs):
    x_refs, w_ref, out_refs, ordered = refs[:4], refs[4], refs[5:-1], refs[-1]
    part = out_refs[0].shape[2]
    tile = min(TILE_N, part)
    order_rows(x_refs, ordered)
    for chunk in range(len(out_refs) // 2):
        for first in range(0, part, tile):
            pair = out_refs[2 * chunk : 2 * chunk + 2]
            multiply(ordered, w_ref, chunk * part + first, tile, pair, first)


def project_far(pieces, weight):
    shifts, _, _, slot_rows, _ = pieces[0].shape
    depth, width = weight.shape
    rows = 8 * shifts * slot_rows
    shape = jax.ShapeDtypeStruct((4, shifts * slot_rows, width // CHUNKS), jnp.bfloat16)
    vmem = pl.BlockSpec(memory_space=pltpu.VMEM)
    return pl.pallas_call(
        far_kernel,
        in_specs=[vmem] * 5,
        out_specs=[vmem] * (2 * CHUNKS),
        scratch_shapes=[pltpu.VMEM((rows, depth), jnp.bfloat16)],
        out_shape=[shape] * (2 * CHUNKS),
        compiler_params=pltpu.CompilerParams(vmem_limit_bytes=24 * MIB),
        cost_estimate=pl.CostEstimate(
            flops=2 * rows * depth * width, bytes_accessed=2 * depth * width, transcendentals=0
        ),
        name="project_far",
    )(*pieces, weight)


def swap(value, distance):
    devices = lax.axis_size("tile")
    return lax.ppermute(value, "tile", [(i, i ^ distance) for i in range(devices)])


def widen(value):
    return value.astype(jnp.float32)


def direct(total):
    sent = total.astype(jnp.bfloat16)
    arrived = [swap(sent[i], 2 * i) for i in range(1, 4)]
    return total[0] + sum(widen(value) for value in arrived)


def stepwise(total):
    total = total.reshape((2, 2) + total.shape[1:])
    total = total[:, 0] + widen(swap(total[:, 1].astype(jnp.bfloat16), 2))
    return total[0] + widen(swap(total[1].astype(jnp.bfloat16), 4))


def per_device(queries, fresh_kv, cache, lengths, out_weight):
    slots = cache.shape[1]
    devices = lax.axis_size("tile")
    cols = devices // GRID_ROWS
    col_width = out_weight.shape[2]
    slot_rows = DECODE_STEPS * slots
    own = lax.axis_index("tile")
    own_block = own // GRID_ROWS
    own_square = own // 2 % 4
    own_core = own % 2

    def send(value, shift, distance):
        def target(i):
            block, row = i // GRID_ROWS, i % GRID_ROWS
            return (block + shift) % cols * GRID_ROWS + (row ^ distance)

        return lax.ppermute(value, "tile", [(i, target(i)) for i in range(devices)])

    attended = attend(queries, fresh_kv, cache, lengths)
    blocks = attended.reshape(slots, KVH, DECODE_STEPS, GROUP // BLOCK_HEADS, BLOCK_HEADS, HD)
    blocks = jnp.transpose(blocks, (3, 1, 4, 2, 0, 5))
    blocks = blocks.reshape(2, 4, BLOCK_HEADS, slot_rows, HD)
    kept = jnp.where(own_core == 0, blocks[0], blocks[1])
    given = jnp.where(own_core == 0, blocks[1], blocks[0])
    cat = jnp.stack([kept, swap(given, 1)], axis=1)
    cat, weight = lax.optimization_barrier((cat, out_weight))
    cat = [
        lax.dynamic_index_in_dim(cat, jnp.bitwise_xor(own_square, distance), 0, False)
        for distance in range(4)
    ]
    far = [
        jnp.stack([send(cat[i], shift, 2 * i) for shift in range(1, cols)]) for i in range(4)
    ]
    near = [(send(cat[i], 0, 2 * i) if i else cat[0])[None] for i in range(4)]
    near_keep, near_give, weight = project_near(near, weight)
    far, weight = lax.optimization_barrier((far, weight))
    partial = project_far(far, weight)
    near_total = widen(near_keep) + widen(swap(near_give, 1))
    backs = []
    for chunk in range(CHUNKS):
        keep, give = partial[2 * chunk : 2 * chunk + 2]
        sums = direct(widen(keep) + widen(swap(give, 1))).astype(jnp.bfloat16)
        sums = sums.reshape(cols - 1, slot_rows, -1)
        backs.append(jnp.stack([send(sums[s - 1], cols - s, 0) for s in range(1, cols)]))
    near = direct(near_total).astype(jnp.bfloat16)
    stacked = jnp.concatenate([near[None], jnp.concatenate(backs, axis=-1)])
    blocks = [
        lax.dynamic_index_in_dim(stacked, lax.rem(j - own_block + cols, cols), 0, False)
        for j in range(cols)
    ]
    return jnp.concatenate(blocks, axis=-1).reshape(DECODE_STEPS, slots, cols * col_width)


def solution(mesh):
    return jax.shard_map(
        per_device,
        mesh=mesh,
        in_specs=(
            P(None, ("groups", "tile"), None),
            P(None, None, ("groups", "tile"), None),
            P(None, ("groups", "tile"), None, None),
            P(("groups", "tile")),
            P("tile", None, None),
        ),
        out_specs=P(None, ("groups", "tile"), None),
        check_vma=False,
    )
```

```python
import functools
import math

import jax
import jax.numpy as jnp
from jax import lax
from jax.experimental import pallas as pl
from jax.experimental.pallas import tpu as pltpu
from jax.sharding import PartitionSpec as P

QH = 64
KVH = 4
HD = 128
DECODE_STEPS = 2
GRID_ROWS = 8
GROUP = QH // KVH
BLOCK_HEADS = QH // GRID_ROWS
CHUNKS = 1
SENDS = 2
TILE_N = 1024
PAGE = 128
TOGETHER = 4
NEAR_GRANT = 24
MIB = 1 << 20


def attention_kernel(
    lengths_ref, query_ref, fresh_ref, cache_ref, out_ref, cached, lengths, fresh, sems, small_sems
):
    slots, capacity, width = cached.shape[1:]
    factor = 1.0 / math.sqrt(HD)
    rows = KVH * DECODE_STEPS * GROUP
    head_rows = rows // KVH
    pages = capacity // PAGE

    def copy(which, slot, page):
        span = pl.ds(page * PAGE, PAGE)
        return pltpu.make_async_copy(
            cache_ref.at[which, slot, span], cached.at[which, slot, span], sems.at[which, slot, page]
        )

    def page_copies(slot, first, used, act):
        for page in range(first, pages):

            @pl.when(page < used)
            def _(page=page):
                for which in range(2):
                    act(copy(which, slot, page))

    lengths_copy = pltpu.make_async_copy(lengths_ref, lengths, small_sems.at[0])
    fresh_copy = pltpu.make_async_copy(fresh_ref, fresh, small_sems.at[1])
    lengths_copy.start()
    fresh_copy.start()
    for slot in range(slots):
        for which in range(2):
            copy(which, slot, 0).start()
    lengths_copy.wait()

    def used_pages(group):
        longest = lengths[group[0]]
        for slot in group[1:]:
            longest = jnp.maximum(longest, lengths[slot])
        used = (longest + DECODE_STEPS + PAGE - 1) // PAGE
        return jnp.where(used >= 3, pages, used)

    groups = [range(first, first + TOGETHER) for first in range(0, slots, TOGETHER)]
    for group in groups:
        used = used_pages(group)
        for slot in group:
            page_copies(slot, 1, used, lambda copy: copy.start())
    own = (
        lax.broadcasted_iota(jnp.int32, (rows, width), 0) // head_rows
        == lax.broadcasted_iota(jnp.int32, (rows, width), 1) // HD
    )
    window_row = lax.broadcasted_iota(jnp.int32, (32, width), 0)
    fresh_copy.wait()

    def patch(slot):
        length = lengths[slot]
        base = pl.multiple_of(jnp.minimum((length // 16) * 16, capacity - 32), 16)
        for which in range(2):
            window = cached[which, slot, pl.ds(base, 32), :].astype(jnp.float32)
            for t in range(DECODE_STEPS):
                row = fresh[t, which].astype(jnp.float32)[slot : slot + 1]
                window = jnp.where(window_row + base == length + t, row, window)
            cached[which, slot, pl.ds(base, 32), :] = window.astype(jnp.bfloat16)

    def mix(group, count):
        position = lax.broadcasted_iota(jnp.int32, (rows, count), 1)
        step = lax.broadcasted_iota(jnp.int32, (rows, count), 0) // GROUP % DECODE_STEPS
        visible = position - step
        scores = []
        for slot in group:
            query = jnp.concatenate([query_ref[slot]] * KVH, axis=1)
            query = jnp.where(own, query, jnp.zeros((), query.dtype))
            scores.append(
                lax.dot_general(
                    query,
                    cached[0, slot, :count, :],
                    (((1,), (1,)), ((), ())),
                    preferred_element_type=jnp.float32,
                )
            )
        weights = []
        for slot, score in zip(group, scores):
            score = jnp.where(visible <= lengths[slot], score * factor, -jnp.inf)
            weight = jnp.exp(score - score.max(-1, keepdims=True))
            weights.append(weight * (1.0 / weight.sum(-1, keepdims=True)))
        for slot, weight in zip(group, weights):
            mixed = jnp.dot(
                weight.astype(jnp.bfloat16),
                cached[1, slot, :count, :],
                preferred_element_type=jnp.float32,
            )
            for head in range(KVH):
                own_rows = slice(head * head_rows, (head + 1) * head_rows)
                own_lanes = slice(head * HD, (head + 1) * HD)
                out_ref[slot, own_rows, :] = mixed[own_rows, own_lanes].astype(jnp.bfloat16)

    for group in groups:
        used = used_pages(group)
        for slot in group:
            for which in range(2):
                copy(which, slot, 0).wait()
            page_copies(slot, 1, used, lambda copy: copy.wait())
        for slot in group:
            patch(slot)
        for count in (1, 2, pages):
            pl.when(used == count)(functools.partial(mix, group, count * PAGE))


def in_hbm(array):
    return pltpu.with_memory_space_constraint(array, pltpu.HBM)


def attend(queries, fresh_kv, cache, lengths):
    slots, capacity, width = cache.shape[1:]
    rows = KVH * DECODE_STEPS * GROUP
    query = queries.reshape(DECODE_STEPS, slots, KVH, GROUP, HD)
    query = jnp.transpose(query, (1, 2, 0, 3, 4)).reshape(slots, rows, HD)
    vmem = pl.BlockSpec(memory_space=pltpu.VMEM)
    hbm = pl.BlockSpec(memory_space=pltpu.HBM)
    return pl.pallas_call(
        attention_kernel,
        out_shape=jax.ShapeDtypeStruct((slots, rows, HD), jnp.bfloat16),
        in_specs=[hbm, vmem, hbm, hbm],
        out_specs=vmem,
        scratch_shapes=[
            pltpu.VMEM((2, slots, capacity, width), jnp.bfloat16),
            pltpu.SMEM(lengths.shape, lengths.dtype),
            pltpu.VMEM(fresh_kv.shape, fresh_kv.dtype),
            pltpu.SemaphoreType.DMA((2, slots, capacity // PAGE)),
            pltpu.SemaphoreType.DMA((2,)),
        ],
        compiler_params=pltpu.CompilerParams(vmem_limit_bytes=40 * MIB),
        name="attention",
    )(in_hbm(lengths), query, in_hbm(fresh_kv), in_hbm(cache))


def order_rows(x_refs, ordered):
    row = 0
    for core in range(2):
        for x_ref in x_refs:
            shifts, _, _, slot_rows, _ = x_ref.shape
            for shift in range(shifts):
                for head in range(BLOCK_HEADS):
                    ordered[row : row + slot_rows, head * HD : (head + 1) * HD] = x_ref[
                        shift, core, head
                    ]
                row += slot_rows


def multiply(ordered, w_ref, start, tile, out_refs, first):
    product = jnp.dot(
        ordered[...], w_ref[:, start : start + tile], preferred_element_type=jnp.float32
    ).astype(jnp.bfloat16)
    half = ordered.shape[0] // 2
    for i, out_ref in enumerate(out_refs):
        out_ref[:, :, first : first + tile] = product[i * half : (i + 1) * half].reshape(
            out_ref.shape[:2] + (tile,)
        )


def near_kernel(*refs):
    x_refs, source_ref = refs[:4], refs[4]
    out_refs, held_ref, ordered, sems = refs[5:7], refs[7], refs[8], refs[9]
    width = held_ref.shape[1]
    tile = width // sems.shape[0]

    def copy(i):
        span = pl.ds(i * tile, tile)
        return pltpu.make_async_copy(source_ref.at[0, :, span], held_ref.at[:, span], sems.at[i])

    for i in range(sems.shape[0]):
        copy(i).start()
    order_rows(x_refs, ordered)
    for i in range(sems.shape[0]):
        copy(i).wait()
        multiply(ordered, held_ref, i * tile, tile, out_refs, i * tile)


def project_near(pieces, weight):
    shifts, _, _, slot_rows, _ = pieces[0].shape
    _, depth, width = weight.shape
    shape = jax.ShapeDtypeStruct((4, shifts * slot_rows, width), jnp.bfloat16)
    vmem = pl.BlockSpec(memory_space=pltpu.VMEM)
    return pl.pallas_call(
        near_kernel,
        in_specs=[vmem] * 4 + [pl.BlockSpec(memory_space=pl.ANY)],
        out_specs=[vmem] * 3,
        scratch_shapes=[
            pltpu.VMEM((8 * shifts * slot_rows, depth), jnp.bfloat16),
            pltpu.SemaphoreType.DMA((max(1, width // TILE_N),)),
        ],
        out_shape=[shape] * 2 + [jax.ShapeDtypeStruct((depth, width), weight.dtype)],
        compiler_params=pltpu.CompilerParams(vmem_limit_bytes=NEAR_GRANT * MIB),
        cost_estimate=pl.CostEstimate(
            flops=16 * shifts * slot_rows * depth * width,
            bytes_accessed=4 * depth * width,
            transcendentals=0,
        ),
        name="project_near",
    )(*pieces, in_hbm(weight))


def far_kernel(*refs):
    x_refs, w_ref, out_refs, ordered = refs[:4], refs[4], refs[5:-1], refs[-1]
    part = out_refs[0].shape[2]
    tile = min(TILE_N, part)
    order_rows(x_refs, ordered)
    for chunk in range(len(out_refs) // 2):
        for first in range(0, part, tile):
            pair = out_refs[2 * chunk : 2 * chunk + 2]
            multiply(ordered, w_ref, chunk * part + first, tile, pair, first)


def project_far(pieces, weight):
    shifts, _, _, slot_rows, _ = pieces[0].shape
    depth, width = weight.shape
    rows = 8 * shifts * slot_rows
    shape = jax.ShapeDtypeStruct((4, shifts * slot_rows, width // CHUNKS), jnp.bfloat16)
    vmem = pl.BlockSpec(memory_space=pltpu.VMEM)
    return pl.pallas_call(
        far_kernel,
        in_specs=[vmem] * 5,
        out_specs=[vmem] * (2 * CHUNKS),
        scratch_shapes=[pltpu.VMEM((rows, depth), jnp.bfloat16)],
        out_shape=[shape] * (2 * CHUNKS),
        compiler_params=pltpu.CompilerParams(vmem_limit_bytes=24 * MIB),
        cost_estimate=pl.CostEstimate(
            flops=2 * rows * depth * width, bytes_accessed=2 * depth * width, transcendentals=0
        ),
        name="project_far",
    )(*pieces, weight)


def swap(value, distance):
    devices = lax.axis_size("tile")
    return lax.ppermute(value, "tile", [(i, i ^ distance) for i in range(devices)])


def widen(value):
    return value.astype(jnp.float32)


def pair_sums(keep, arrived):
    sums = [widen(keep[i]) + widen(arrived[i]) for i in range(4)]
    return sums[0], [value.astype(jnp.bfloat16) for value in sums[1:]]


def direct(own, sent):
    arrived = [swap(value, 2 * (i + 1)) for i, value in enumerate(sent)]
    return (own + sum(widen(value) for value in arrived)).astype(jnp.bfloat16)


def per_device(queries, fresh_kv, cache, lengths, out_weight):
    slots = cache.shape[1]
    devices = lax.axis_size("tile")
    cols = devices // GRID_ROWS
    col_width = out_weight.shape[2]
    slot_rows = DECODE_STEPS * slots
    own = lax.axis_index("tile")
    own_block = own // GRID_ROWS
    own_square = own // 2 % 4
    own_core = own % 2

    def send(value, shift, distance):
        def target(i):
            block, row = i // GRID_ROWS, i % GRID_ROWS
            return (block + shift) % cols * GRID_ROWS + (row ^ distance)

        return lax.ppermute(value, "tile", [(i, target(i)) for i in range(devices)])

    attended = attend(queries, fresh_kv, cache, lengths)
    blocks = attended.reshape(slots, KVH, DECODE_STEPS, GROUP // BLOCK_HEADS, BLOCK_HEADS, HD)
    blocks = jnp.transpose(blocks, (3, 1, 4, 2, 0, 5))
    blocks = blocks.reshape(2, 4, BLOCK_HEADS, slot_rows, HD)
    kept = jnp.where(own_core == 0, blocks[0], blocks[1])
    given = jnp.where(own_core == 0, blocks[1], blocks[0])
    cat = jnp.stack([kept, swap(given, 1)], axis=1)
    cat, weight = lax.optimization_barrier((cat, out_weight))
    cat = [
        lax.dynamic_index_in_dim(cat, jnp.bitwise_xor(own_square, distance), 0, False)
        for distance in range(4)
    ]
    far = [
        jnp.stack([send(cat[i], shift, 2 * i) for shift in range(1, cols)]) for i in range(4)
    ]
    near = [(send(cat[i], 0, 2 * i) if i else cat[0])[None] for i in range(4)]
    near_keep, near_give, weight = project_near(near, weight)
    far, weight, near_give = lax.optimization_barrier((far, weight, near_give))
    partial = project_far(far, weight)
    near = pair_sums(near_keep, swap(near_give, 1))
    far = pair_sums(partial[0], swap(partial[1], 1))
    far, near = lax.optimization_barrier((far, near))
    backs = []
    width = col_width // SENDS
    for first in range(0, col_width, width):
        lanes = slice(first, first + width)
        sums = direct(far[0][:, lanes], [value[:, lanes] for value in far[1]])
        sums = sums.reshape(cols - 1, slot_rows, -1)
        backs.append(jnp.stack([send(sums[s - 1], cols - s, 0) for s in range(1, cols)]))
    near = direct(*near)
    stacked = jnp.concatenate([near[None], jnp.concatenate(backs, axis=-1)])
    blocks = [
        lax.dynamic_index_in_dim(stacked, lax.rem(j - own_block + cols, cols), 0, False)
        for j in range(cols)
    ]
    return jnp.concatenate(blocks, axis=-1).reshape(DECODE_STEPS, slots, cols * col_width)


def solution(mesh):
    return jax.shard_map(
        per_device,
        mesh=mesh,
        in_specs=(
            P(None, ("groups", "tile"), None),
            P(None, None, ("groups", "tile"), None),
            P(None, ("groups", "tile"), None, None),
            P(("groups", "tile")),
            P("tile", None, None),
        ),
        out_specs=P(None, ("groups", "tile"), None),
        check_vma=False,
    )
```

```python
import functools
import math

import jax
import jax.numpy as jnp
from jax import lax
from jax.experimental import pallas as pl
from jax.experimental.pallas import tpu as pltpu
from jax.sharding import PartitionSpec as P

QH = 64
KVH = 4
HD = 128
DECODE_STEPS = 2
GRID_ROWS = 8
GROUP = QH // KVH
BLOCK_HEADS = QH // GRID_ROWS
CHUNKS = 1
SENDS = 1
TILE_N = 1024
PAGE = 128
TOGETHER = 4
NEAR_GRANT = 24
MIB = 1 << 20


def attention_kernel(
    lengths_ref, query_ref, fresh_ref, cache_ref, out_ref, cached, lengths, fresh, sems, small_sems
):
    slots, capacity, width = cached.shape[1:]
    factor = 1.0 / math.sqrt(HD)
    rows = KVH * DECODE_STEPS * GROUP
    head_rows = rows // KVH
    pages = capacity // PAGE

    def copy(which, slot, page):
        span = pl.ds(page * PAGE, PAGE)
        return pltpu.make_async_copy(
            cache_ref.at[which, slot, span], cached.at[which, slot, span], sems.at[which, slot, page]
        )

    def page_copies(slot, first, used, act):
        for page in range(first, pages):

            @pl.when(page < used)
            def _(page=page):
                for which in range(2):
                    act(copy(which, slot, page))

    lengths_copy = pltpu.make_async_copy(lengths_ref, lengths, small_sems.at[0])
    fresh_copy = pltpu.make_async_copy(fresh_ref, fresh, small_sems.at[1])
    lengths_copy.start()
    fresh_copy.start()
    for slot in range(slots):
        for which in range(2):
            copy(which, slot, 0).start()
    lengths_copy.wait()

    def used_pages(group):
        longest = lengths[group[0]]
        for slot in group[1:]:
            longest = jnp.maximum(longest, lengths[slot])
        used = (longest + DECODE_STEPS + PAGE - 1) // PAGE
        return jnp.where(used >= 3, pages, used)

    groups = [range(first, first + TOGETHER) for first in range(0, slots, TOGETHER)]
    for group in groups:
        used = used_pages(group)
        for slot in group:
            page_copies(slot, 1, used, lambda copy: copy.start())
    own = (
        lax.broadcasted_iota(jnp.int32, (rows, width), 0) // head_rows
        == lax.broadcasted_iota(jnp.int32, (rows, width), 1) // HD
    )
    window_row = lax.broadcasted_iota(jnp.int32, (32, width), 0)
    fresh_copy.wait()

    def patch(slot):
        length = lengths[slot]
        base = pl.multiple_of(jnp.minimum((length // 16) * 16, capacity - 32), 16)
        for which in range(2):
            window = cached[which, slot, pl.ds(base, 32), :].astype(jnp.float32)
            for t in range(DECODE_STEPS):
                row = fresh[t, which].astype(jnp.float32)[slot : slot + 1]
                window = jnp.where(window_row + base == length + t, row, window)
            cached[which, slot, pl.ds(base, 32), :] = window.astype(jnp.bfloat16)

    def mix(group, count):
        position = lax.broadcasted_iota(jnp.int32, (rows, count), 1)
        step = lax.broadcasted_iota(jnp.int32, (rows, count), 0) // GROUP % DECODE_STEPS
        visible = position - step
        scores = []
        for slot in group:
            query = jnp.concatenate([query_ref[slot]] * KVH, axis=1)
            query = jnp.where(own, query, jnp.zeros((), query.dtype))
            scores.append(
                lax.dot_general(
                    query,
                    cached[0, slot, :count, :],
                    (((1,), (1,)), ((), ())),
                    preferred_element_type=jnp.float32,
                )
            )
        weights = []
        for slot, score in zip(group, scores):
            score = jnp.where(visible <= lengths[slot], score * factor, -jnp.inf)
            weight = jnp.exp(score - score.max(-1, keepdims=True))
            weights.append(weight * (1.0 / weight.sum(-1, keepdims=True)))
        for slot, weight in zip(group, weights):
            mixed = jnp.dot(
                weight.astype(jnp.bfloat16),
                cached[1, slot, :count, :],
                preferred_element_type=jnp.float32,
            )
            for head in range(KVH):
                own_rows = slice(head * head_rows, (head + 1) * head_rows)
                own_lanes = slice(head * HD, (head + 1) * HD)
                out_ref[slot, own_rows, :] = mixed[own_rows, own_lanes].astype(jnp.bfloat16)

    for group in groups:
        used = used_pages(group)
        for slot in group:
            for which in range(2):
                copy(which, slot, 0).wait()
            page_copies(slot, 1, used, lambda copy: copy.wait())
        for slot in group:
            patch(slot)
        for count in (1, 2, pages):
            pl.when(used == count)(functools.partial(mix, group, count * PAGE))


def in_hbm(array):
    return pltpu.with_memory_space_constraint(array, pltpu.HBM)


def attend(queries, fresh_kv, cache, lengths):
    slots, capacity, width = cache.shape[1:]
    rows = KVH * DECODE_STEPS * GROUP
    query = queries.reshape(DECODE_STEPS, slots, KVH, GROUP, HD)
    query = jnp.transpose(query, (1, 2, 0, 3, 4)).reshape(slots, rows, HD)
    vmem = pl.BlockSpec(memory_space=pltpu.VMEM)
    hbm = pl.BlockSpec(memory_space=pltpu.HBM)
    return pl.pallas_call(
        attention_kernel,
        out_shape=jax.ShapeDtypeStruct((slots, rows, HD), jnp.bfloat16),
        in_specs=[hbm, vmem, hbm, hbm],
        out_specs=vmem,
        scratch_shapes=[
            pltpu.VMEM((2, slots, capacity, width), jnp.bfloat16),
            pltpu.SMEM(lengths.shape, lengths.dtype),
            pltpu.VMEM(fresh_kv.shape, fresh_kv.dtype),
            pltpu.SemaphoreType.DMA((2, slots, capacity // PAGE)),
            pltpu.SemaphoreType.DMA((2,)),
        ],
        compiler_params=pltpu.CompilerParams(vmem_limit_bytes=40 * MIB),
        name="attention",
    )(in_hbm(lengths), query, in_hbm(fresh_kv), in_hbm(cache))


def order_rows(x_refs, ordered):
    row = 0
    for core in range(2):
        for x_ref in x_refs:
            shifts, _, _, slot_rows, _ = x_ref.shape
            for shift in range(shifts):
                for head in range(BLOCK_HEADS):
                    ordered[row : row + slot_rows, head * HD : (head + 1) * HD] = x_ref[
                        shift, core, head
                    ]
                row += slot_rows


def multiply(ordered, w_ref, start, tile, out_refs, first):
    product = jnp.dot(
        ordered[...], w_ref[:, start : start + tile], preferred_element_type=jnp.float32
    ).astype(jnp.bfloat16)
    half = ordered.shape[0] // 2
    for i, out_ref in enumerate(out_refs):
        out_ref[:, :, first : first + tile] = product[i * half : (i + 1) * half].reshape(
            out_ref.shape[:2] + (tile,)
        )


def near_kernel(*refs):
    x_refs, source_ref = refs[:4], refs[4]
    out_refs, held_ref, ordered, sems = refs[5:7], refs[7], refs[8], refs[9]
    width = held_ref.shape[1]
    tile = width // sems.shape[0]

    def copy(i):
        span = pl.ds(i * tile, tile)
        return pltpu.make_async_copy(source_ref.at[0, :, span], held_ref.at[:, span], sems.at[i])

    for i in range(sems.shape[0]):
        copy(i).start()
    order_rows(x_refs, ordered)
    for i in range(sems.shape[0]):
        copy(i).wait()
        multiply(ordered, held_ref, i * tile, tile, out_refs, i * tile)


def project_near(pieces, weight):
    shifts, _, _, slot_rows, _ = pieces[0].shape
    _, depth, width = weight.shape
    shape = jax.ShapeDtypeStruct((4, shifts * slot_rows, width), jnp.bfloat16)
    vmem = pl.BlockSpec(memory_space=pltpu.VMEM)
    return pl.pallas_call(
        near_kernel,
        in_specs=[vmem] * 4 + [pl.BlockSpec(memory_space=pl.ANY)],
        out_specs=[vmem] * 3,
        scratch_shapes=[
            pltpu.VMEM((8 * shifts * slot_rows, depth), jnp.bfloat16),
            pltpu.SemaphoreType.DMA((max(1, width // TILE_N),)),
        ],
        out_shape=[shape] * 2 + [jax.ShapeDtypeStruct((depth, width), weight.dtype)],
        compiler_params=pltpu.CompilerParams(vmem_limit_bytes=NEAR_GRANT * MIB),
        cost_estimate=pl.CostEstimate(
            flops=16 * shifts * slot_rows * depth * width,
            bytes_accessed=4 * depth * width,
            transcendentals=0,
        ),
        name="project_near",
    )(*pieces, in_hbm(weight))


def far_kernel(*refs):
    x_refs, w_ref, out_refs, ordered = refs[:4], refs[4], refs[5:-1], refs[-1]
    part = out_refs[0].shape[2]
    tile = min(TILE_N, part)
    order_rows(x_refs, ordered)
    for chunk in range(len(out_refs) // 2):
        for first in range(0, part, tile):
            pair = out_refs[2 * chunk : 2 * chunk + 2]
            multiply(ordered, w_ref, chunk * part + first, tile, pair, first)


def project_far(pieces, weight):
    shifts, _, _, slot_rows, _ = pieces[0].shape
    depth, width = weight.shape
    rows = 8 * shifts * slot_rows
    shape = jax.ShapeDtypeStruct((4, shifts * slot_rows, width // CHUNKS), jnp.bfloat16)
    vmem = pl.BlockSpec(memory_space=pltpu.VMEM)
    return pl.pallas_call(
        far_kernel,
        in_specs=[vmem] * 5,
        out_specs=[vmem] * (2 * CHUNKS),
        scratch_shapes=[pltpu.VMEM((rows, depth), jnp.bfloat16)],
        out_shape=[shape] * (2 * CHUNKS),
        compiler_params=pltpu.CompilerParams(vmem_limit_bytes=24 * MIB),
        cost_estimate=pl.CostEstimate(
            flops=2 * rows * depth * width, bytes_accessed=2 * depth * width, transcendentals=0
        ),
        name="project_far",
    )(*pieces, weight)


def swap(value, distance):
    devices = lax.axis_size("tile")
    return lax.ppermute(value, "tile", [(i, i ^ distance) for i in range(devices)])


def widen(value):
    return value.astype(jnp.float32)


def pair_sums(keep, arrived):
    sums = [widen(keep[i]) + widen(arrived[i]) for i in range(4)]
    return sums[0], [value.astype(jnp.bfloat16) for value in sums[1:]]


def direct(own, sent):
    arrived = [swap(value, 2 * (i + 1)) for i, value in enumerate(sent)]
    return (own + sum(widen(value) for value in arrived)).astype(jnp.bfloat16)


def per_device(queries, fresh_kv, cache, lengths, out_weight):
    slots = cache.shape[1]
    devices = lax.axis_size("tile")
    cols = devices // GRID_ROWS
    col_width = out_weight.shape[2]
    slot_rows = DECODE_STEPS * slots
    own = lax.axis_index("tile")
    own_block = own // GRID_ROWS
    own_square = own // 2 % 4
    own_core = own % 2

    def send(value, shift, distance):
        def target(i):
            block, row = i // GRID_ROWS, i % GRID_ROWS
            return (block + shift) % cols * GRID_ROWS + (row ^ distance)

        return lax.ppermute(value, "tile", [(i, target(i)) for i in range(devices)])

    attended = attend(queries, fresh_kv, cache, lengths)
    blocks = attended.reshape(slots, KVH, DECODE_STEPS, GROUP // BLOCK_HEADS, BLOCK_HEADS, HD)
    blocks = jnp.transpose(blocks, (3, 1, 4, 2, 0, 5))
    blocks = blocks.reshape(2, 4, BLOCK_HEADS, slot_rows, HD)
    kept = jnp.where(own_core == 0, blocks[0], blocks[1])
    given = jnp.where(own_core == 0, blocks[1], blocks[0])
    cat = jnp.stack([kept, swap(given, 1)], axis=1)
    cat, weight = lax.optimization_barrier((cat, out_weight))
    cat = [
        lax.dynamic_index_in_dim(cat, jnp.bitwise_xor(own_square, distance), 0, False)
        for distance in range(4)
    ]
    far = [
        jnp.stack([send(cat[i], shift, 2 * i) for shift in range(1, cols)]) for i in range(4)
    ]
    near = [(send(cat[i], 0, 2 * i) if i else cat[0])[None] for i in range(4)]
    near_keep, near_give, weight = project_near(near, weight)
    far, weight, near_give = lax.optimization_barrier((far, weight, near_give))
    partial = project_far(far, weight)
    near = pair_sums(near_keep, swap(near_give, 1))
    far = pair_sums(partial[0], swap(partial[1], 1))
    far, near = lax.optimization_barrier((far, near))
    near = direct(*near)
    backs = []
    width = col_width // SENDS
    for first in range(0, col_width, width):
        lanes = slice(first, first + width)
        sums = direct(far[0][:, lanes], [value[:, lanes] for value in far[1]])
        sums = sums.reshape(cols - 1, slot_rows, -1)
        backs.append(jnp.stack([send(sums[s - 1], cols - s, 0) for s in range(1, cols)]))
    stacked = jnp.concatenate([near[None], jnp.concatenate(backs, axis=-1)])
    blocks = [
        lax.dynamic_index_in_dim(stacked, lax.rem(j - own_block + cols, cols), 0, False)
        for j in range(cols)
    ]
    return jnp.concatenate(blocks, axis=-1).reshape(DECODE_STEPS, slots, cols * col_width)


def solution(mesh):
    return jax.shard_map(
        per_device,
        mesh=mesh,
        in_specs=(
            P(None, ("groups", "tile"), None),
            P(None, None, ("groups", "tile"), None),
            P(None, ("groups", "tile"), None, None),
            P(("groups", "tile")),
            P("tile", None, None),
        ),
        out_specs=P(None, ("groups", "tile"), None),
        check_vma=False,
    )
```
